32 devices in a mesh: grp: 2 (over x), quad: 2 (over core), box: 8 (over z, y).
Axes of the slice: x: 2, y: 2, z: 4, core: 2. Of those that a mesh axis runs over, the one named last changes fastest.
Arguments:
- charges: float32 [4, 256, 64, 512], P(('grp', 'quad'), 'box'), parts along dimension 0, may hold values from -6 to 6
- src_factors: bfloat16 [4, 2, 64, 256, 256], P(('grp', 'quad'), None, 'box'), parts along dimension 0, may hold values from -0.375 to 0.375
- tgt_factors: bfloat16 [4, 1, 64, 256, 256], P(('grp', 'quad'), None, 'box'), parts along dimension 0, may hold values from -0.375 to 0.375
- leaf_factors: bfloat16 [128, 256, 256], P(('grp', 'box')), parts along dimension 0, may hold values from -0.375 to 0.375
- src_connect: int32 [2, 2, 256], P('quad', None, 'box'), may hold values from 0 to 255, as said below
- tgt_connect: int32 [2, 256], P(None, 'box'), may hold values from 0 to 255, as said below
Outputs:
- potentials: float32 [512, 64, 512], P(('grp', 'box'), None, 'quad'), parts along dimension 0
The draws below stay inside these ranges and needn't reach their ends.
There are 2 independent parts, one for each index of `grp`. The reference program is written for one: setup_inputs(seed, part) draws one part's arguments, and reference() takes and returns one part's arrays. A program takes and returns all parts, laid end to end along the dimension named above; an argument that names none is the same for every part. Nothing has to cross between parts.
Inputs may be any that keep to these rules, and one draw needn't show every extreme that they name: `src_connect`: each aligned block of 32 entries of a row is a permutation of that block's own positions in the row. `tgt_connect`: each aligned block of 32 entries of a row is a permutation of that block's own positions in the row.
All inputs are finite; a program needn't handle non-finite values.
Results may differ from the reference program's by a relative error of at most 0.0003.
Values may be sent and summed in bfloat16 or wider, within the bound.
A program may use at most 64 MiB of HBM per device.

```python
import jax
import jax.numpy as jnp
from jax import lax

K = 64
FACT = 256
R = 512
NODE_DEV = 32
LS = 2
LT = 2
QUADS = 2
NODES = 256
N_BOX = 8


def block_shuffles(key, row_count):
    key_list = jax.random.split(key, row_count * N_BOX)
    shuffles = jax.vmap(lambda one_key: jax.random.permutation(one_key, NODE_DEV))(key_list)
    offsets = jnp.arange(N_BOX, dtype=jnp.int32) * NODE_DEV
    shuffles = shuffles.astype(jnp.int32).reshape(row_count, N_BOX, NODE_DEV) + offsets[None, :, None]
    return shuffles.reshape(row_count, NODES).astype(jnp.int32)


def draw_src_connect(key, part):
    key = jax.random.fold_in(key, 11)
    return block_shuffles(key, QUADS * LS).reshape(QUADS, LS, NODES)


def draw_tgt_connect(key, part):
    key = jax.random.fold_in(key, 12)
    return block_shuffles(key, LT)


def level_of(stream_key, extent, cuts, low, largest):
    loudness = 1.0
    for axis_at, shards_of in cuts:
        steps = jax.random.uniform(jax.random.fold_in(jax.random.fold_in(stream_key, 6), axis_at), (shards_of,), jnp.float32, low / len(cuts), largest / len(cuts))
        loudness = loudness * jnp.repeat(jnp.exp(steps), extent[axis_at] // shards_of).reshape((-1,) + (1,) * (len(extent) - 1 - axis_at))
    return loudness


def centred(stream_key, shape, deviation, limit, cuts=(), held_as=jnp.bfloat16):
    array = deviation * jax.random.normal(stream_key, shape, jnp.float32)
    if cuts:
        array = array * level_of(stream_key, shape, cuts, -0.22, 0.18)
    return jnp.clip(array, -limit, limit).astype(held_as)


def setup_inputs(seed: int = 0, part: int = 0) -> dict:
    key_of = jax.random.split(jax.random.key(seed), 7)
    own_keys = jax.random.split(jax.random.fold_in(key_of[6], part), 7)
    return {
        "charges": centred(own_keys[0], (QUADS, NODES, K, R), 1.0, 6.0, ((0, 2), (1, 8)), jnp.float32),
        "src_factors": centred(own_keys[1], (QUADS, LS, NODES // 4, FACT, FACT), FACT ** -0.5, 0.375, ((0, 2), (2, 8))),
        "tgt_factors": centred(own_keys[2], (QUADS, LT - 1, NODES // 4, FACT, FACT), FACT ** -0.5, 0.375, ((0, 2), (2, 8))),
        "leaf_factors": centred(own_keys[3], (NODES // 4, FACT, FACT), FACT ** -0.5, 0.375, ((0, 8),)),
        "src_connect": draw_src_connect(jax.random.fold_in(key_of[6], 71), part),
        "tgt_connect": draw_tgt_connect(jax.random.fold_in(key_of[6], 71), part),
    }


def apply_level(current, connect, factors):
    node_count, rank_size, col_count = current.shape
    gathered = jnp.take(current, connect, axis=0).reshape(node_count // 4, 4 * rank_size, col_count)
    result = jnp.einsum("gij,gjc->gic", factors.astype(jnp.float32), gathered, precision=lax.Precision.HIGHEST)
    return result.reshape(node_count, rank_size, col_count)


def transpose_owners(current):
    node_count, rank_size, col_count = current.shape
    per_peer = node_count // (N_BOX * N_BOX)
    split_view = current.reshape(N_BOX, N_BOX, per_peer, rank_size, col_count)
    return jnp.transpose(split_view, (1, 0, 2, 3, 4)).reshape(node_count, rank_size, col_count)


def reference(charges, src_factors, tgt_factors, leaf_factors, src_connect, tgt_connect):
    summed = jnp.zeros(charges.shape[1:], jnp.float32)
    for quadrant in range(QUADS):
        current = charges[quadrant]
        for level_index in range(LS):
            current = apply_level(current, src_connect[quadrant, level_index], src_factors[quadrant, level_index])
        current = transpose_owners(current)
        for level_index in range(LT - 1):
            current = apply_level(current, tgt_connect[level_index], tgt_factors[quadrant, level_index])
        summed = summed + current
    return apply_level(summed, tgt_connect[LT - 1], leaf_factors)
```

```python
import functools

import jax
import jax.numpy as jnp
from jax import lax
from jax.experimental import pallas as pl
from jax.experimental.pallas import tpu as pltpu
from jax.sharding import PartitionSpec as P

MESH = pl.DeviceIdType.MESH
WIDTH = 128
LARGEST = 32767.0
ROUNDER = 12582912.0
SMALLEST = 1e-33


def partner(me, step, count):
    if count & (count - 1):
        return lax.rem(me + step, count)
    other = 0
    bit = 1
    while bit < count:
        mine = lax.rem(lax.div(me, bit), 2)
        theirs = lax.rem(lax.div(step, bit), 2)
        other = other + bit * (mine + theirs - 2 * mine * theirs)
        bit *= 2
    return other


def product(factor, values):
    high = values.astype(jnp.bfloat16)
    low = (values - high.astype(jnp.float32)).astype(jnp.bfloat16)
    return jnp.dot(factor, high, preferred_element_type=jnp.float32) + jnp.dot(
        factor, low, preferred_element_type=jnp.float32
    )


def kernel(cfg, src_con, tgt_con, charges, src_f, tgt_f, leaf_f, out, *scratch):
    boxes, quads, nodes, rank, per, chunks, levels, share, unit = cfg
    steps = chunks * quads
    groups = nodes // per
    scales = share // unit
    take = iter(scratch)
    held = [next(take) for _ in range(steps)]
    sent = [next(take) for _ in range(steps)]
    sent_scale = [next(take) for _ in range(steps)]
    got = [next(take) for _ in range(chunks)]
    got_scale = [next(take) for _ in range(chunks)]
    done = [next(take) for _ in range(chunks)]
    work, middle, src_v, tgt_v, leaf_v = [next(take) for _ in range(5)]
    (held_sem, src_sem, tgt_sem, leaf_sem, own_sem, out_sem,
     swap_send, swap_recv, send, recv, scale_send, scale_recv) = list(take)

    grp = lax.axis_index("grp")
    quad = lax.axis_index("quad")
    box = lax.axis_index("box")

    def quad_at(ahead):
        return lax.rem(quad + ahead, quads)

    def device(ahead, other):
        return {"grp": grp, "quad": quad_at(ahead), "box": other}

    barrier = pltpu.get_barrier_semaphore()
    for ahead in range(quads):
        for d in range(boxes):
            if ahead or d:
                pl.semaphore_signal(
                    barrier, inc=1, device_id=device(ahead, partner(box, d, boxes)),
                    device_id_type=MESH,
                )

    half = chunks * WIDTH
    loads = []
    for s in range(steps):
        c, ahead = s // quads, s % quads
        column = pl.multiple_of(quad_at(ahead) * half + c * WIDTH, WIDTH)
        loads.append(pltpu.make_async_copy(
            charges.at[0, :, :, pl.ds(column, WIDTH)], held[s], held_sem.at[s]))
    src_loads = [
        pltpu.make_async_copy(src_f.at[0, l], src_v.at[l], src_sem.at[l]) for l in range(levels)
    ]
    tgt_load = pltpu.make_async_copy(tgt_f.at[0, 0], tgt_v.at[0], tgt_sem)
    leaf_load = pltpu.make_async_copy(leaf_f, leaf_v, leaf_sem)
    loads[0].start()
    for load in src_loads + loads[1:] + [tgt_load, leaf_load]:
        load.start()

    def gather(read, connect, g):
        return jnp.concatenate(
            [read(lax.rem(connect(per * g + k), nodes)) for k in range(per)], axis=0
        )

    def source(s):
        for l in range(levels):
            before = held[s] if l == 0 else work.at[(l - 1) % 2]

            def body(g, carry, l=l):
                values = gather(
                    (lambda i: held[s][i]) if l == 0 else (lambda i: work[(l - 1) % 2, i]),
                    lambda slot: src_con[0, l, slot], g,
                )
                result = product(src_v[l, g], values)
                if l < levels - 1:
                    work[l % 2, pl.ds(per * g, per)] = result.reshape(per, rank, WIDTH)
                else:
                    parts = result.reshape(per // unit, unit * rank, WIDTH)
                    top = jnp.maximum(
                        jnp.max(jnp.abs(parts), axis=1, keepdims=True), SMALLEST)
                    sent_scale[s][pl.ds(per // unit * g, per // unit)] = top * (1.0 / LARGEST)
                    whole = (parts * (LARGEST / top) + ROUNDER) - ROUNDER
                    sent[s][pl.ds(per * g, per)] = (
                        whole.astype(jnp.int32).astype(jnp.int16).reshape(per, rank, WIDTH))
                return carry

            lax.fori_loop(0, groups, body, 0, unroll=2)

    def copies(s, d):
        c, ahead = s // quads, s % quads
        other = partner(box, d, boxes)
        at = dict(device_id=device(ahead, other), device_id_type=MESH)
        return (
            pltpu.make_async_remote_copy(
                src_ref=sent[s].at[pl.ds(other * share, share)],
                dst_ref=got[c].at[ahead, pl.ds(box * share, share)],
                send_sem=send.at[c, ahead, d], recv_sem=recv.at[c, ahead, d], **at),
            pltpu.make_async_remote_copy(
                src_ref=sent_scale[s].at[pl.ds(other * scales, scales)],
                dst_ref=got_scale[c].at[ahead, pl.ds(box * scales, scales)],
                send_sem=scale_send.at[c, ahead, d], recv_sem=scale_recv.at[c, ahead, d], **at),
        )

    def own_copies(c):
        s = c * quads
        return (
            pltpu.make_async_copy(
                sent[s].at[pl.ds(box * share, share)],
                got[c].at[0, pl.ds(box * share, share)], own_sem.at[c, 0]),
            pltpu.make_async_copy(
                sent_scale[s].at[pl.ds(box * scales, scales)],
                got_scale[c].at[0, pl.ds(box * scales, scales)], own_sem.at[c, 1]),
        )

    def each(s, act):
        first = 0 if s % quads else 1

        def body(n, carry):
            for copy in copies(s, boxes - 1 - n):
                act(copy)
            return carry

        lax.fori_loop(0, boxes - first, body, 0)

    swaps = [
        pltpu.make_async_remote_copy(
            src_ref=tgt_f.at[0, 0], dst_ref=tgt_v.at[ahead],
            send_sem=swap_send.at[ahead], recv_sem=swap_recv.at[ahead],
            device_id=device(ahead, box), device_id_type=MESH)
        for ahead in range(1, quads)
    ]

    for s in range(steps):
        loads[s].wait()
        if s == 0:
            for load in src_loads:
                load.wait()
        source(s)
        if s == 0:
            pl.semaphore_wait(barrier, boxes * quads - 1)
        each(s, lambda copy: copy.start())
        if s % quads == 0:
            for copy in own_copies(s // quads):
                copy.start()
        if s == 0:
            for swap in swaps:
                swap.start()

    tgt_load.wait()
    leaf_load.wait()
    for swap in swaps:
        swap.wait()
    stores = []
    for c in range(chunks):
        for ahead in range(quads):
            each(c * quads + ahead, lambda copy: copy.wait_recv())
        for copy in own_copies(c):
            copy.wait()

        def target(g, carry, c=c):
            total = None
            for ahead in range(quads):
                def read(i, ahead=ahead):
                    return got[c][ahead, i].astype(jnp.int32).astype(jnp.float32) * (
                        got_scale[c][ahead, lax.div(i, unit)])
                term = product(tgt_v[ahead, g], gather(read, lambda slot: tgt_con[0, slot], g))
                total = term if total is None else total + term
            middle[pl.ds(per * g, per)] = total.reshape(per, rank, WIDTH)
            return carry

        lax.fori_loop(0, groups, target, 0, unroll=2)

        def leaf(g, carry, c=c):
            values = gather(lambda i: middle[i], lambda slot: tgt_con[1, slot], g)
            done[c][pl.ds(per * g, per)] = product(leaf_v[g], values).reshape(per, rank, WIDTH)
            return carry

        lax.fori_loop(0, groups, leaf, 0, unroll=2)
        store = pltpu.make_async_copy(
            done[c], out.at[:, :, pl.ds(c * WIDTH, WIDTH)], out_sem.at[c])
        store.start()
        stores.append(store)

    for s in range(steps):
        each(s, lambda copy: copy.wait_send())
    for store in stores:
        store.wait()


def per_device(mesh, charges, src_factors, tgt_factors, leaf_factors, src_connect, tgt_connect):
    boxes, quads = mesh.shape["box"], mesh.shape["quad"]
    _, nodes, rank, columns = charges.shape
    levels, groups, fact = src_factors.shape[1:4]
    per = fact // rank
    share = nodes // boxes
    unit = min(share, per)
    chunks = columns // quads // WIDTH
    steps = chunks * quads
    slab = (nodes, rank, WIDTH)
    cfg = (boxes, quads, nodes, rank, per, chunks, levels, share, unit)
    dma = pltpu.SemaphoreType.DMA
    scratch = (
        [pltpu.VMEM(slab, jnp.float32)] * steps
        + [pltpu.VMEM(slab, jnp.int16)] * steps
        + [pltpu.VMEM((nodes // unit, 1, WIDTH), jnp.float32)] * steps
        + [pltpu.VMEM((quads,) + slab, jnp.int16)] * chunks
        + [pltpu.VMEM((quads, nodes // unit, 1, WIDTH), jnp.float32)] * chunks
        + [pltpu.VMEM(slab, jnp.float32)] * chunks
        + [
            pltpu.VMEM((2,) + slab, jnp.float32),
            pltpu.VMEM(slab, jnp.float32),
            pltpu.VMEM((levels, groups, fact, fact), jnp.bfloat16),
            pltpu.VMEM((quads, groups, fact, fact), jnp.bfloat16),
            pltpu.VMEM((groups, fact, fact), jnp.bfloat16),
            dma((steps,)), dma((levels,)), dma, dma, dma((chunks, 2)), dma((chunks,)),
            dma((quads,)), dma((quads,)),
        ]
        + [dma((chunks, quads, boxes))] * 4
    )
    smem = pl.BlockSpec(memory_space=pltpu.SMEM)
    anywhere = pl.BlockSpec(memory_space=pl.ANY)
    flops = 2 * (levels + 1) * groups * fact * fact * columns
    return pl.pallas_call(
        functools.partial(kernel, cfg),
        out_shape=jax.ShapeDtypeStruct((nodes, rank, columns // quads), jnp.float32),
        in_specs=[smem, smem, anywhere, anywhere, anywhere, anywhere],
        out_specs=anywhere,
        scratch_shapes=scratch,
        compiler_params=pltpu.CompilerParams(
            collective_id=0, has_side_effects=True, vmem_limit_bytes=48 * 2**20
        ),
        cost_estimate=pl.CostEstimate(flops=flops, bytes_accessed=10 * 2**20, transcendentals=0),
    )(src_connect, tgt_connect, charges, src_factors, tgt_factors, leaf_factors)


def solution(mesh):
    placed = (
        P(("grp", "quad"), "box", None, None),
        P(("grp", "quad"), None, "box", None, None),
        P(("grp", "quad"), None, "box", None, None),
        P(("grp", "box"), None, None),
        P("quad", None, "box"),
        P(None, "box"),
    )
    return jax.shard_map(
        functools.partial(per_device, mesh),
        mesh=mesh,
        in_specs=placed,
        out_specs=P(("grp", "box"), None, "quad"),
        check_vma=False,
    )
```

```python
import functools

import jax
import jax.numpy as jnp
from jax import lax
from jax.experimental import pallas as pl
from jax.experimental.pallas import tpu as pltpu
from jax.sharding import PartitionSpec as P

MESH = pl.DeviceIdType.MESH
WIDTH = 128
LARGEST = 32767.0
ROUNDER = 12582912.0
SMALLEST = 1e-33


def partner(me, step, count):
    if count & (count - 1):
        return lax.rem(me + step, count)
    other = 0
    bit = 1
    while bit < count:
        mine = lax.rem(lax.div(me, bit), 2)
        theirs = lax.rem(lax.div(step, bit), 2)
        other = other + bit * (mine + theirs - 2 * mine * theirs)
        bit *= 2
    return other


def product(factor, values):
    high = values.astype(jnp.bfloat16)
    low = (values - high.astype(jnp.float32)).astype(jnp.bfloat16)
    return jnp.dot(factor, high, preferred_element_type=jnp.float32) + jnp.dot(
        factor, low, preferred_element_type=jnp.float32
    )


def kernel(cfg, src_hbm, tgt_hbm, charges, src_f, tgt_f, leaf_f, out, *scratch):
    boxes, quads, nodes, rank, per, chunks, levels, share, unit = cfg
    steps = chunks * quads
    groups = nodes // per
    scales = share // unit
    take = iter(scratch)
    held = [next(take) for _ in range(steps)]
    sent = [next(take) for _ in range(steps)]
    sent_scale = [next(take) for _ in range(steps)]
    got = [next(take) for _ in range(chunks)]
    got_scale = [next(take) for _ in range(chunks)]
    done = [next(take) for _ in range(chunks)]
    work, middle, src_v, tgt_v, leaf_v, src_con, tgt_con = [next(take) for _ in range(7)]
    (con_sem, held_sem, src_sem, tgt_sem, leaf_sem, own_sem, out_sem,
     swap_send, swap_recv, send, recv, scale_send, scale_recv) = list(take)

    grp = lax.axis_index("grp")
    quad = lax.axis_index("quad")
    box = lax.axis_index("box")

    def quad_at(ahead):
        return lax.rem(quad + ahead, quads)

    def device(ahead, other):
        return {"grp": grp, "quad": quad_at(ahead), "box": other}

    half = chunks * WIDTH
    loads = []
    for s in range(steps):
        c, ahead = s // quads, s % quads
        column = pl.multiple_of(quad_at(ahead) * half + c * WIDTH, WIDTH)
        loads.append(pltpu.make_async_copy(
            charges.at[0, :, :, pl.ds(column, WIDTH)], held[s], held_sem.at[s]))
    src_loads = [
        pltpu.make_async_copy(src_f.at[0, l], src_v.at[l], src_sem.at[l]) for l in range(levels)
    ]
    tgt_load = pltpu.make_async_copy(tgt_f.at[0, 0], tgt_v.at[0], tgt_sem)
    leaf_load = pltpu.make_async_copy(leaf_f, leaf_v, leaf_sem)
    con_loads = [
        pltpu.make_async_copy(src_hbm, src_con, con_sem.at[0]),
        pltpu.make_async_copy(tgt_hbm, tgt_con, con_sem.at[1]),
    ]
    for load in con_loads + [loads[0]] + src_loads:
        load.start()

    barrier = pltpu.get_barrier_semaphore()
    for ahead in range(quads):
        for d in range(boxes):
            if ahead or d:
                pl.semaphore_signal(
                    barrier, inc=1, device_id=device(ahead, partner(box, d, boxes)),
                    device_id_type=MESH,
                )

    def gather(read, connect, g):
        return jnp.concatenate(
            [read(lax.rem(connect(per * g + k), nodes)) for k in range(per)], axis=0
        )

    def source(s):
        for l in range(levels):
            def body(g, carry, l=l):
                values = gather(
                    (lambda i: held[s][i]) if l == 0 else (lambda i: work[(l - 1) % 2, i]),
                    lambda slot: src_con[0, l, slot], g,
                )
                result = product(src_v[l, g], values)
                if l < levels - 1:
                    work[l % 2, pl.ds(per * g, per)] = result.reshape(per, rank, WIDTH)
                else:
                    parts = result.reshape(per // unit, unit * rank, WIDTH)
                    top = jnp.maximum(
                        jnp.max(jnp.abs(parts), axis=1, keepdims=True), SMALLEST)
                    sent_scale[s][pl.ds(per // unit * g, per // unit)] = top * (1.0 / LARGEST)
                    whole = (parts * (LARGEST / top) + ROUNDER) - ROUNDER
                    sent[s][pl.ds(per * g, per)] = (
                        whole.astype(jnp.int32).astype(jnp.int16).reshape(per, rank, WIDTH))
                return carry

            lax.fori_loop(0, groups, body, 0, unroll=True)

    def copies(s, d):
        c, ahead = s // quads, s % quads
        other = partner(box, d, boxes)
        at = dict(device_id=device(ahead, other), device_id_type=MESH)
        return (
            pltpu.make_async_remote_copy(
                src_ref=sent[s].at[pl.ds(other * share, share)],
                dst_ref=got[c].at[ahead, pl.ds(box * share, share)],
                send_sem=send.at[c, ahead, d], recv_sem=recv.at[c, ahead, d], **at),
            pltpu.make_async_remote_copy(
                src_ref=sent_scale[s].at[pl.ds(other * scales, scales)],
                dst_ref=got_scale[c].at[ahead, pl.ds(box * scales, scales)],
                send_sem=scale_send.at[c, ahead, d], recv_sem=scale_recv.at[c, ahead, d], **at),
        )

    def own_copies(c):
        s = c * quads
        return (
            pltpu.make_async_copy(
                sent[s].at[pl.ds(box * share, share)],
                got[c].at[0, pl.ds(box * share, share)], own_sem.at[c, 0]),
            pltpu.make_async_copy(
                sent_scale[s].at[pl.ds(box * scales, scales)],
                got_scale[c].at[0, pl.ds(box * scales, scales)], own_sem.at[c, 1]),
        )

    def each(s, act):
        first = 0 if s % quads else 1

        def body(n, carry):
            for copy in copies(s, n + first):
                act(copy)
            return carry

        lax.fori_loop(0, boxes - first, body, 0)

    swaps = [
        pltpu.make_async_remote_copy(
            src_ref=tgt_f.at[0, 0], dst_ref=tgt_v.at[ahead],
            send_sem=swap_send.at[ahead], recv_sem=swap_recv.at[ahead],
            device_id=device(ahead, box), device_id_type=MESH)
        for ahead in range(1, quads)
    ]

    for s in range(steps):
        loads[s].wait()
        if s == 0:
            for load in con_loads + src_loads:
                load.wait()
            for load in loads[1:] + [tgt_load, leaf_load]:
                load.start()
        source(s)
        if s == 0:
            pl.semaphore_wait(barrier, boxes * quads - 1)
        each(s, lambda copy: copy.start())
        if s % quads == 0:
            for copy in own_copies(s // quads):
                copy.start()
        if s == 0:
            for swap in swaps:
                swap.start()

    tgt_load.wait()
    leaf_load.wait()
    for swap in swaps:
        swap.wait()
    stores = []
    for c in range(chunks):
        for ahead in range(quads):
            each(c * quads + ahead, lambda copy: copy.wait_recv())
        for copy in own_copies(c):
            copy.wait()

        def target(g, carry, c=c):
            total = None
            for ahead in range(quads):
                def read(i, ahead=ahead):
                    return got[c][ahead, i].astype(jnp.int32).astype(jnp.float32) * (
                        got_scale[c][ahead, lax.div(i, unit)])
                term = product(tgt_v[ahead, g], gather(read, lambda slot: tgt_con[0, slot], g))
                total = term if total is None else total + term
            middle[pl.ds(per * g, per)] = total.reshape(per, rank, WIDTH)
            return carry

        lax.fori_loop(0, groups, target, 0, unroll=True)

        def leaf(g, carry, c=c):
            values = gather(lambda i: middle[i], lambda slot: tgt_con[1, slot], g)
            done[c][pl.ds(per * g, per)] = product(leaf_v[g], values).reshape(per, rank, WIDTH)
            return carry

        lax.fori_loop(0, groups, leaf, 0, unroll=True)
        store = pltpu.make_async_copy(
            done[c], out.at[:, :, pl.ds(c * WIDTH, WIDTH)], out_sem.at[c])
        store.start()
        stores.append(store)

    for s in range(steps):
        each(s, lambda copy: copy.wait_send())
    for store in stores:
        store.wait()


def per_device(mesh, charges, src_factors, tgt_factors, leaf_factors, src_connect, tgt_connect):
    boxes, quads = mesh.shape["box"], mesh.shape["quad"]
    _, nodes, rank, columns = charges.shape
    levels, groups, fact = src_factors.shape[1:4]
    per = fact // rank
    share = nodes // boxes
    unit = min(share, per)
    chunks = columns // quads // WIDTH
    steps = chunks * quads
    slab = (nodes, rank, WIDTH)
    cfg = (boxes, quads, nodes, rank, per, chunks, levels, share, unit)
    dma = pltpu.SemaphoreType.DMA
    scratch = (
        [pltpu.VMEM(slab, jnp.float32)] * steps
        + [pltpu.VMEM(slab, jnp.int16)] * steps
        + [pltpu.VMEM((nodes // unit, 1, WIDTH), jnp.float32)] * steps
        + [pltpu.VMEM((quads,) + slab, jnp.int16)] * chunks
        + [pltpu.VMEM((quads, nodes // unit, 1, WIDTH), jnp.float32)] * chunks
        + [pltpu.VMEM(slab, jnp.float32)] * chunks
        + [
            pltpu.VMEM((2,) + slab, jnp.float32),
            pltpu.VMEM(slab, jnp.float32),
            pltpu.VMEM((levels, groups, fact, fact), jnp.bfloat16),
            pltpu.VMEM((quads, groups, fact, fact), jnp.bfloat16),
            pltpu.VMEM((groups, fact, fact), jnp.bfloat16),
            pltpu.SMEM(src_connect.shape, jnp.int32),
            pltpu.SMEM(tgt_connect.shape, jnp.int32),
            dma((2,)), dma((steps,)), dma((levels,)), dma, dma, dma((chunks, 2)), dma((chunks,)),
            dma((quads,)), dma((quads,)),
        ]
        + [dma((chunks, quads, boxes))] * 4
    )
    fixed = pl.BlockSpec(memory_space=pltpu.HBM)
    anywhere = pl.BlockSpec(memory_space=pl.ANY)
    flops = 2 * (levels + 1) * groups * fact * fact * columns
    return pl.pallas_call(
        functools.partial(kernel, cfg),
        out_shape=jax.ShapeDtypeStruct((nodes, rank, columns // quads), jnp.float32),
        in_specs=[fixed] * 6,
        out_specs=anywhere,
        scratch_shapes=scratch,
        compiler_params=pltpu.CompilerParams(
            collective_id=0, has_side_effects=True, vmem_limit_bytes=48 * 2**20
        ),
        cost_estimate=pl.CostEstimate(flops=flops, bytes_accessed=10 * 2**20, transcendentals=0),
    )(src_connect, tgt_connect, charges, src_factors, tgt_factors, leaf_factors)


def solution(mesh):
    placed = (
        P(("grp", "quad"), "box", None, None),
        P(("grp", "quad"), None, "box", None, None),
        P(("grp", "quad"), None, "box", None, None),
        P(("grp", "box"), None, None),
        P("quad", None, "box"),
        P(None, "box"),
    )
    return jax.shard_map(
        functools.partial(per_device, mesh),
        mesh=mesh,
        in_specs=placed,
        out_specs=P(("grp", "box"), None, "quad"),
        check_vma=False,
    )
```

```python
import functools

import jax
import jax.numpy as jnp
from jax import lax
from jax.experimental import pallas as pl
from jax.experimental.pallas import tpu as pltpu
from jax.sharding import PartitionSpec as P

MESH = pl.DeviceIdType.MESH
WIDTH = 128
LARGEST = 32767.0
ROUNDER = 12582912.0
SMALLEST = 1e-33


def partner(me, step, count):
    if count & (count - 1):
        return lax.rem(me + step, count)
    other = 0
    bit = 1
    while bit < count:
        mine = lax.rem(lax.div(me, bit), 2)
        theirs = lax.rem(lax.div(step, bit), 2)
        other = other + bit * (mine + theirs - 2 * mine * theirs)
        bit *= 2
    return other


def product(factor, values):
    high = values.astype(jnp.bfloat16)
    low = (values - high.astype(jnp.float32)).astype(jnp.bfloat16)
    return jnp.dot(factor, high, preferred_element_type=jnp.float32) + jnp.dot(
        factor, low, preferred_element_type=jnp.float32
    )


def kernel(cfg, src_hbm, tgt_hbm, charges, src_f, tgt_f, leaf_f, out, *scratch):
    boxes, quads, nodes, rank, per, chunks, levels, share, unit = cfg
    steps = chunks * quads
    groups = nodes // per
    scales = share // unit
    take = iter(scratch)
    held = [next(take) for _ in range(steps)]
    sent = [next(take) for _ in range(steps)]
    sent_scale = [next(take) for _ in range(steps)]
    got = [next(take) for _ in range(chunks)]
    got_scale = [next(take) for _ in range(chunks)]
    done = [next(take) for _ in range(chunks)]
    work, middle, src_v, tgt_v, leaf_v, src_con, tgt_con = [next(take) for _ in range(7)]
    (con_sem, held_sem, src_sem, tgt_sem, leaf_sem, own_sem, out_sem,
     swap_send, swap_recv, send, recv, scale_send, scale_recv) = list(take)

    grp = lax.axis_index("grp")
    quad = lax.axis_index("quad")
    box = lax.axis_index("box")

    def quad_at(ahead):
        return lax.rem(quad + ahead, quads)

    def device(ahead, other):
        return {"grp": grp, "quad": quad_at(ahead), "box": other}

    half = chunks * WIDTH
    loads = []
    for s in range(steps):
        c, ahead = s // quads, s % quads
        column = pl.multiple_of(quad_at(ahead) * half + c * WIDTH, WIDTH)
        loads.append(pltpu.make_async_copy(
            charges.at[0, :, :, pl.ds(column, WIDTH)], held[s], held_sem.at[s]))
    src_loads = [
        pltpu.make_async_copy(src_f.at[0, l], src_v.at[l], src_sem.at[l]) for l in range(levels)
    ]
    tgt_load = pltpu.make_async_copy(tgt_f.at[0, 0], tgt_v.at[0], tgt_sem)
    leaf_load = pltpu.make_async_copy(leaf_f, leaf_v, leaf_sem)
    con_loads = [
        pltpu.make_async_copy(src_hbm, src_con, con_sem.at[0]),
        pltpu.make_async_copy(tgt_hbm, tgt_con, con_sem.at[1]),
    ]
    for load in con_loads + [loads[0]] + src_loads:
        load.start()

    barrier = pltpu.get_barrier_semaphore()
    for ahead in range(quads):
        for d in range(boxes):
            if ahead or d:
                pl.semaphore_signal(
                    barrier, inc=1, device_id=device(ahead, partner(box, d, boxes)),
                    device_id_type=MESH,
                )

    def gather(read, connect, g):
        return jnp.concatenate(
            [read(lax.rem(connect(per * g + k), nodes)) for k in range(per)], axis=0
        )

    def source(s):
        for l in range(levels):
            def body(g, carry, l=l):
                values = gather(
                    (lambda i: held[s][i]) if l == 0 else (lambda i: work[(l - 1) % 2, i]),
                    lambda slot: src_con[0, l, slot], g,
                )
                result = product(src_v[l, g], values)
                if l < levels - 1:
                    work[l % 2, pl.ds(per * g, per)] = result.reshape(per, rank, WIDTH)
                else:
                    parts = result.reshape(per // unit, unit * rank, WIDTH)
                    top = jnp.maximum(
                        jnp.max(jnp.abs(parts), axis=1, keepdims=True), SMALLEST)
                    sent_scale[s][pl.ds(per // unit * g, per // unit)] = top * (1.0 / LARGEST)
                    whole = (parts * (LARGEST / top) + ROUNDER) - ROUNDER
                    sent[s][pl.ds(per * g, per)] = (
                        whole.astype(jnp.int32).astype(jnp.int16).reshape(per, rank, WIDTH))
                return carry

            lax.fori_loop(0, groups, body, 0, unroll=True)

    def copies(s, d):
        c, ahead = s // quads, s % quads
        other = partner(box, d, boxes)
        at = dict(device_id=device(ahead, other), device_id_type=MESH)
        return (
            pltpu.make_async_remote_copy(
                src_ref=sent[s].at[pl.ds(other * share, share)],
                dst_ref=got[c].at[ahead, pl.ds(box * share, share)],
                send_sem=send.at[c, ahead, d], recv_sem=recv.at[c, ahead, d], **at),
            pltpu.make_async_remote_copy(
                src_ref=sent_scale[s].at[pl.ds(other * scales, scales)],
                dst_ref=got_scale[c].at[ahead, pl.ds(box * scales, scales)],
                send_sem=scale_send.at[c, ahead, d], recv_sem=scale_recv.at[c, ahead, d], **at),
        )

    def own_copies(c):
        s = c * quads
        return (
            pltpu.make_async_copy(
                sent[s].at[pl.ds(box * share, share)],
                got[c].at[0, pl.ds(box * share, share)], own_sem.at[c, 0]),
            pltpu.make_async_copy(
                sent_scale[s].at[pl.ds(box * scales, scales)],
                got_scale[c].at[0, pl.ds(box * scales, scales)], own_sem.at[c, 1]),
        )

    def each(s, act):
        first = 0 if s % quads else 1

        def body(n, carry):
            for copy in copies(s, n + first):
                act(copy)
            return carry

        lax.fori_loop(0, boxes - first, body, 0)

    swaps = [
        pltpu.make_async_remote_copy(
            src_ref=tgt_f.at[0, 0], dst_ref=tgt_v.at[ahead],
            send_sem=swap_send.at[ahead], recv_sem=swap_recv.at[ahead],
            device_id=device(ahead, box), device_id_type=MESH)
        for ahead in range(1, quads)
    ]

    for s in range(steps):
        loads[s].wait()
        if s == 0:
            for load in con_loads + src_loads:
                load.wait()
            for load in loads[1:] + [tgt_load, leaf_load]:
                load.start()
        source(s)
        if s == 0:
            pl.semaphore_wait(barrier, boxes * quads - 1)
        each(s, lambda copy: copy.start())
        if s % quads == 0:
            for copy in own_copies(s // quads):
                copy.start()
        if s == 0:
            for swap in swaps:
                swap.start()

    tgt_load.wait()
    leaf_load.wait()
    for swap in swaps:
        swap.wait()
    stores = []
    for c in range(chunks):
        for ahead in range(quads):
            each(c * quads + ahead, lambda copy: copy.wait_recv())
        for copy in own_copies(c):
            copy.wait()

        def target(g, carry, c=c):
            total = None
            for ahead in range(quads):
                def read(i, ahead=ahead):
                    return got[c][ahead, i].astype(jnp.int32).astype(jnp.float32) * (
                        got_scale[c][ahead, lax.div(i, unit)])
                term = product(tgt_v[ahead, g], gather(read, lambda slot: tgt_con[0, slot], g))
                total = term if total is None else total + term
            middle[pl.ds(per * g, per)] = total.reshape(per, rank, WIDTH)
            return carry

        lax.fori_loop(0, groups, target, 0, unroll=True)

        def leaf(g, carry, c=c):
            values = gather(lambda i: middle[i], lambda slot: tgt_con[1, slot], g)
            done[c][pl.ds(per * g, per)] = product(leaf_v[g], values).reshape(per, rank, WIDTH)
            return carry

        lax.fori_loop(0, groups, leaf, 0, unroll=True)
        store = pltpu.make_async_copy(
            done[c], out.at[:, :, pl.ds(c * WIDTH, WIDTH)], out_sem.at[c])
        store.start()
        stores.append(store)

    for s in range(steps):
        each(s, lambda copy: copy.wait_send())
    for store in stores:
        store.wait()


def per_device(mesh, charges, src_factors, tgt_factors, leaf_factors, src_connect, tgt_connect):
    boxes, quads = mesh.shape["box"], mesh.shape["quad"]
    _, nodes, rank, columns = charges.shape
    levels, groups, fact = src_factors.shape[1:4]
    per = fact // rank
    share = nodes // boxes
    unit = min(share, per)
    chunks = columns // quads // WIDTH
    steps = chunks * quads
    slab = (nodes, rank, WIDTH)
    cfg = (boxes, quads, nodes, rank, per, chunks, levels, share, unit)
    dma = pltpu.SemaphoreType.DMA
    scratch = (
        [pltpu.VMEM(slab, jnp.float32)] * steps
        + [pltpu.VMEM(slab, jnp.int16)] * steps
        + [pltpu.VMEM((nodes // unit, 1, WIDTH), jnp.float32)] * steps
        + [pltpu.VMEM((quads,) + slab, jnp.int16)] * chunks
        + [pltpu.VMEM((quads, nodes // unit, 1, WIDTH), jnp.float32)] * chunks
        + [pltpu.VMEM(slab, jnp.float32)] * chunks
        + [
            pltpu.VMEM((2,) + slab, jnp.float32),
            pltpu.VMEM(slab, jnp.float32),
            pltpu.VMEM((levels, groups, fact, fact), jnp.bfloat16),
            pltpu.VMEM((quads, groups, fact, fact), jnp.bfloat16),
            pltpu.VMEM((groups, fact, fact), jnp.bfloat16),
            pltpu.SMEM(src_connect.shape, jnp.int32),
            pltpu.SMEM(tgt_connect.shape, jnp.int32),
            dma((2,)), dma((steps,)), dma((levels,)), dma, dma, dma((chunks, 2)), dma((chunks,)),
            dma((quads,)), dma((quads,)),
        ]
        + [dma((chunks, quads, boxes))] * 4
    )
    fixed = pl.BlockSpec(memory_space=pltpu.HBM)
    anywhere = pl.BlockSpec(memory_space=pl.ANY)
    flops = 2 * (levels + 1) * groups * fact * fact * columns
    return pl.pallas_call(
        functools.partial(kernel, cfg),
        out_shape=jax.ShapeDtypeStruct((nodes, rank, columns // quads), jnp.float32),
        in_specs=[fixed] * 6,
        out_specs=anywhere,
        scratch_shapes=scratch,
        compiler_params=pltpu.CompilerParams(
            collective_id=0, has_side_effects=True, vmem_limit_bytes=48 * 2**20
        ),
        cost_estimate=pl.CostEstimate(flops=flops, bytes_accessed=10 * 2**20, transcendentals=0),
    )(*(
        pltpu.with_memory_space_constraint(array, pltpu.HBM)
        for array in (src_connect, tgt_connect, charges, src_factors, tgt_factors, leaf_factors)
    ))


def solution(mesh):
    placed = (
        P(("grp", "quad"), "box", None, None),
        P(("grp", "quad"), None, "box", None, None),
        P(("grp", "quad"), None, "box", None, None),
        P(("grp", "box"), None, None),
        P("quad", None, "box"),
        P(None, "box"),
    )
    return jax.shard_map(
        functools.partial(per_device, mesh),
        mesh=mesh,
        in_specs=placed,
        out_specs=P(("grp", "box"), None, "quad"),
        check_vma=False,
    )
```

```python
import functools

import jax
import jax.numpy as jnp
from jax import lax
from jax.experimental import pallas as pl
from jax.experimental.pallas import tpu as pltpu
from jax.sharding import PartitionSpec as P

MESH = pl.DeviceIdType.MESH
WIDTH = 128
LARGEST = 32767.0
ROUNDER = 12582912.0
SMALLEST = 1e-33


def partner(me, step, count):
    if count & (count - 1):
        return lax.rem(me + step, count)
    other = 0
    bit = 1
    while bit < count:
        mine = lax.rem(lax.div(me, bit), 2)
        theirs = lax.rem(lax.div(step, bit), 2)
        other = other + bit * (mine + theirs - 2 * mine * theirs)
        bit *= 2
    return other


def product(factor, values):
    high = values.astype(jnp.bfloat16)
    low = (values - high.astype(jnp.float32)).astype(jnp.bfloat16)
    return jnp.dot(factor, high, preferred_element_type=jnp.float32) + jnp.dot(
        factor, low, preferred_element_type=jnp.float32
    )


def kernel(cfg, src_hbm, tgt_hbm, charges, src_f, tgt_f, leaf_f, out, *scratch):
    boxes, quads, nodes, rank, per, chunks, levels, share, unit = cfg
    steps = chunks * quads
    groups = nodes // per
    scales = share // unit
    take = iter(scratch)
    held = [next(take) for _ in range(steps)]
    sent = [next(take) for _ in range(steps)]
    sent_scale = [next(take) for _ in range(steps)]
    got = [[next(take) for _ in range(quads)] for _ in range(chunks)]
    got_scale = [[next(take) for _ in range(quads)] for _ in range(chunks)]
    done = [next(take) for _ in range(chunks)]
    work, middle, src_v, tgt_v, leaf_v, src_con, tgt_con = [next(take) for _ in range(7)]
    (con_sem, held_sem, src_sem, tgt_sem, leaf_sem, own_sem, out_sem,
     swap_send, swap_recv, send, recv, scale_send, scale_recv) = list(take)

    grp = lax.axis_index("grp")
    quad = lax.axis_index("quad")
    box = lax.axis_index("box")

    def quad_at(ahead):
        return lax.rem(quad + ahead, quads)

    def device(ahead, other):
        return {"grp": grp, "quad": quad_at(ahead), "box": other}

    half = chunks * WIDTH
    loads = []
    for s in range(steps):
        c, ahead = s // quads, s % quads
        column = pl.multiple_of(quad_at(ahead) * half + c * WIDTH, WIDTH)
        loads.append(pltpu.make_async_copy(
            charges.at[0, :, :, pl.ds(column, WIDTH)], held[s], held_sem.at[s]))
    src_loads = [
        pltpu.make_async_copy(src_f.at[0, l], src_v.at[l], src_sem.at[l]) for l in range(levels)
    ]
    tgt_load = pltpu.make_async_copy(tgt_f.at[0, 0], tgt_v.at[0], tgt_sem)
    leaf_load = pltpu.make_async_copy(leaf_f, leaf_v, leaf_sem)
    con_loads = [
        pltpu.make_async_copy(src_hbm, src_con, con_sem.at[0]),
        pltpu.make_async_copy(tgt_hbm, tgt_con, con_sem.at[1]),
    ]
    for load in con_loads + [loads[0]] + src_loads:
        load.start()

    barrier = pltpu.get_barrier_semaphore()
    for ahead in range(quads):
        for d in range(boxes):
            if ahead or d:
                pl.semaphore_signal(
                    barrier, inc=1, device_id=device(ahead, partner(box, d, boxes)),
                    device_id_type=MESH,
                )

    def gather(read, connect, g):
        return jnp.concatenate(
            [read(lax.rem(connect(per * g + k), nodes)) for k in range(per)], axis=0
        )

    def source(s):
        for l in range(levels):
            def body(g, carry, l=l):
                values = gather(
                    (lambda i: held[s][i]) if l == 0 else (lambda i: work[(l - 1) % 2, i]),
                    lambda slot: src_con[0, l, slot], g,
                )
                result = product(src_v[l, g], values)
                if l < levels - 1:
                    work[l % 2, pl.ds(per * g, per)] = result.reshape(per, rank, WIDTH)
                else:
                    parts = result.reshape(per // unit, unit * rank, WIDTH)
                    top = jnp.maximum(
                        jnp.max(jnp.abs(parts), axis=1, keepdims=True), SMALLEST)
                    sent_scale[s][pl.ds(per // unit * g, per // unit)] = top * (1.0 / LARGEST)
                    whole = (parts * (LARGEST / top) + ROUNDER) - ROUNDER
                    sent[s][pl.ds(per * g, per)] = (
                        whole.astype(jnp.int32).astype(jnp.int16).reshape(per, rank, WIDTH))
                return carry

            lax.fori_loop(0, groups, body, 0, unroll=True)

    def copies(s, d):
        c, ahead = s // quads, s % quads
        other = partner(box, d, boxes)
        at = dict(device_id=device(ahead, other), device_id_type=MESH)
        return (
            pltpu.make_async_remote_copy(
                src_ref=sent[s].at[pl.ds(other * share, share)],
                dst_ref=got[c][ahead].at[pl.ds(box * share, share)],
                send_sem=send.at[c, ahead, d], recv_sem=recv.at[c, ahead, d], **at),
            pltpu.make_async_remote_copy(
                src_ref=sent_scale[s].at[pl.ds(other * scales, scales)],
                dst_ref=got_scale[c][ahead].at[pl.ds(box * scales, scales)],
                send_sem=scale_send.at[c, ahead, d], recv_sem=scale_recv.at[c, ahead, d], **at),
        )

    def own_copies(c):
        s = c * quads
        return (
            pltpu.make_async_copy(
                sent[s].at[pl.ds(box * share, share)],
                got[c][0].at[pl.ds(box * share, share)], own_sem.at[c, 0]),
            pltpu.make_async_copy(
                sent_scale[s].at[pl.ds(box * scales, scales)],
                got_scale[c][0].at[pl.ds(box * scales, scales)], own_sem.at[c, 1]),
        )

    def each(s, act):
        first = 0 if s % quads else 1

        def body(n, carry):
            for copy in copies(s, n + first):
                act(copy)
            return carry

        lax.fori_loop(0, boxes - first, body, 0)

    swaps = [
        pltpu.make_async_remote_copy(
            src_ref=tgt_f.at[0, 0], dst_ref=tgt_v.at[ahead],
            send_sem=swap_send.at[ahead], recv_sem=swap_recv.at[ahead],
            device_id=device(ahead, box), device_id_type=MESH)
        for ahead in range(1, quads)
    ]

    for s in range(steps):
        loads[s].wait()
        if s == 0:
            for load in con_loads + src_loads:
                load.wait()
            for load in loads[1:] + [tgt_load, leaf_load]:
                load.start()
        source(s)
        if s == 0:
            pl.semaphore_wait(barrier, boxes * quads - 1)
        each(s, lambda copy: copy.start())
        if s % quads == 0:
            for copy in own_copies(s // quads):
                copy.start()
        if s == 0:
            for swap in swaps:
                swap.start()

    tgt_load.wait()
    leaf_load.wait()
    for swap in swaps:
        swap.wait()
    stores = []
    for c in range(chunks):
        for ahead in range(quads):
            each(c * quads + ahead, lambda copy: copy.wait_recv())
            if ahead == 0:
                for copy in own_copies(c):
                    copy.wait()

            def target(g, carry, c=c, ahead=ahead):
                def read(i):
                    return got[c][ahead][i].astype(jnp.int32).astype(jnp.float32) * (
                        got_scale[c][ahead][lax.div(i, unit)])

                term = product(tgt_v[ahead, g], gather(read, lambda slot: tgt_con[0, slot], g))
                term = term.reshape(per, rank, WIDTH)
                at = pl.ds(per * g, per)
                middle[at] = term if ahead == 0 else middle[at] + term
                return carry

            lax.fori_loop(0, groups, target, 0, unroll=True)

        def leaf(g, carry, c=c):
            values = gather(lambda i: middle[i], lambda slot: tgt_con[1, slot], g)
            done[c][pl.ds(per * g, per)] = product(leaf_v[g], values).reshape(per, rank, WIDTH)
            return carry

        lax.fori_loop(0, groups, leaf, 0, unroll=True)
        store = pltpu.make_async_copy(
            done[c], out.at[:, :, pl.ds(c * WIDTH, WIDTH)], out_sem.at[c])
        store.start()
        stores.append(store)

    for s in range(steps):
        each(s, lambda copy: copy.wait_send())
    for store in stores:
        store.wait()


def per_device(mesh, charges, src_factors, tgt_factors, leaf_factors, src_connect, tgt_connect):
    boxes, quads = mesh.shape["box"], mesh.shape["quad"]
    _, nodes, rank, columns = charges.shape
    levels, groups, fact = src_factors.shape[1:4]
    per = fact // rank
    share = nodes // boxes
    unit = min(share, per)
    chunks = columns // quads // WIDTH
    steps = chunks * quads
    slab = (nodes, rank, WIDTH)
    cfg = (boxes, quads, nodes, rank, per, chunks, levels, share, unit)
    dma = pltpu.SemaphoreType.DMA
    scratch = (
        [pltpu.VMEM(slab, jnp.float32)] * steps
        + [pltpu.VMEM(slab, jnp.int16)] * steps
        + [pltpu.VMEM((nodes // unit, 1, WIDTH), jnp.float32)] * steps
        + [pltpu.VMEM(slab, jnp.int16)] * steps
        + [pltpu.VMEM((nodes // unit, 1, WIDTH), jnp.float32)] * steps
        + [pltpu.VMEM(slab, jnp.float32)] * chunks
        + [
            pltpu.VMEM((2,) + slab, jnp.float32),
            pltpu.VMEM(slab, jnp.float32),
            pltpu.VMEM((levels, groups, fact, fact), jnp.bfloat16),
            pltpu.VMEM((quads, groups, fact, fact), jnp.bfloat16),
            pltpu.VMEM((groups, fact, fact), jnp.bfloat16),
            pltpu.SMEM(src_connect.shape, jnp.int32),
            pltpu.SMEM(tgt_connect.shape, jnp.int32),
            dma((2,)), dma((steps,)), dma((levels,)), dma, dma, dma((chunks, 2)), dma((chunks,)),
            dma((quads,)), dma((quads,)),
        ]
        + [dma((chunks, quads, boxes))] * 4
    )
    fixed = pl.BlockSpec(memory_space=pltpu.HBM)
    anywhere = pl.BlockSpec(memory_space=pl.ANY)
    flops = 2 * (levels + 1) * groups * fact * fact * columns
    return pl.pallas_call(
        functools.partial(kernel, cfg),
        out_shape=jax.ShapeDtypeStruct((nodes, rank, columns // quads), jnp.float32),
        in_specs=[fixed] * 6,
        out_specs=anywhere,
        scratch_shapes=scratch,
        compiler_params=pltpu.CompilerParams(
            collective_id=0, has_side_effects=True, vmem_limit_bytes=48 * 2**20
        ),
        cost_estimate=pl.CostEstimate(flops=flops, bytes_accessed=10 * 2**20, transcendentals=0),
    )(*(
        pltpu.with_memory_space_constraint(array, pltpu.HBM)
        for array in (src_connect, tgt_connect, charges, src_factors, tgt_factors, leaf_factors)
    ))


def solution(mesh):
    placed = (
        P(("grp", "quad"), "box", None, None),
        P(("grp", "quad"), None, "box", None, None),
        P(("grp", "quad"), None, "box", None, None),
        P(("grp", "box"), None, None),
        P("quad", None, "box"),
        P(None, "box"),
    )
    return jax.shard_map(
        functools.partial(per_device, mesh),
        mesh=mesh,
        in_specs=placed,
        out_specs=P(("grp", "box"), None, "quad"),
        check_vma=False,
    )
```
